32 devices in a mesh: series: 16 (over z, y, core), tm: 2 (over x).
Axes of the slice: x: 2, y: 2, z: 4, core: 2. Of those that a mesh axis runs over, the one named last changes fastest.
Arguments:
- data: float32 [16384, 2048], P('series', 'tm'), may hold values from -36 to 36, as said below
- sparse: float32 [16384, 2048], P('series', 'tm'), may hold values from -4 to 4
- omega: bfloat16 [2048, 256], P('tm'), may hold values from -0.125 to 0.125
- svt_scale: float32 [1], replicated, may hold values from 0.6 to 1.2
- sparse_threshold: float32 [1], replicated, may hold values from 0.3 to 1.5
Outputs:
- low_rank: float32 [16384, 2048], P('series', 'tm')
- sparse_new: float32 [16384, 2048], P('series', 'tm')
The draws below stay inside these ranges and needn't reach their ends.
Inputs may be any that keep to these rules, and one draw needn't show every extreme that they name: `data`: each entry is a series scale times a minute scale times a bounded random value.
All inputs are finite; a program needn't handle non-finite values.
Results may differ from the reference program's by a relative error of at most 0.003.
Values sent between devices are 32-bit elements; how exact they have to be, the bound alone decides.
A program may use at most 64 MiB of HBM per device.

```python
import math
import jax
import jax.numpy as jnp
from jax import lax

MIN = 2048
K = 256
ROOT_STEPS = 12
SIGN_STEPS = 12
ROWS = 16384


def draw_data(key, part):
    key = jax.random.fold_in(key, 11)
    first, second, third = jax.random.split(key, 3)
    row_scale = jnp.exp(jax.random.uniform(first, (ROWS, 1), jnp.float32, math.log(0.3), math.log(3.0)))
    col_scale = jnp.exp(jax.random.uniform(second, (1, MIN), jnp.float32, math.log(0.3), math.log(3.0)))
    noise = jax.random.truncated_normal(third, -4.0, 4.0, (ROWS, MIN), jnp.float32)
    return row_scale * col_scale * noise


def block_scale(rng, shape, pieces, least, largest):
    def one(position, parts):
        steps = jax.random.uniform(jax.random.fold_in(jax.random.fold_in(rng, 6), position), (parts,), jnp.float32, least / len(pieces), largest / len(pieces))
        return jnp.repeat(jnp.exp(steps), shape[position] // parts).reshape((-1,) + (1,) * (len(shape) - position - 1))

    gain = one(*pieces[0])
    for cut in pieces[1:]:
        gain = gain * one(*cut)
    return gain


def bell_draw(own_key, shape, spread, limit, cuts=(), kind=jnp.bfloat16):
    loudness = block_scale(own_key, shape, cuts, -0.22, 0.18) if cuts else 1.0
    drawn = jax.random.normal(own_key, shape, jnp.float32) * spread * loudness
    return jnp.minimum(jnp.maximum(drawn, -limit), limit).astype(kind)


def setup_inputs(seed: int = 0) -> dict:
    arg_keys = jax.random.split(jax.random.key(seed), 6)
    return {
        "data": draw_data(jax.random.fold_in(arg_keys[5], 71), 0),
        "sparse": bell_draw(arg_keys[1], (ROWS, MIN), 0.5, 4.0, ((0, 16), (1, 2)), jnp.float32),
        "omega": bell_draw(arg_keys[2], (MIN, K), MIN ** -0.5, 0.125, ((0, 2),)),
        "svt_scale": jnp.clip(jnp.exp(jax.random.uniform(arg_keys[3], (1,), jnp.float32, math.log(0.6), math.log(1.2))), 0.6, 1.2),
        "sparse_threshold": jnp.clip(jnp.exp(jax.random.uniform(arg_keys[4], (1,), jnp.float32, math.log(0.3), math.log(1.5))), 0.3, 1.5),
    }


def shrink_factor(gram, svt_scale):
    highest = lax.Precision.HIGHEST
    columns = gram.shape[0]
    identity = jnp.eye(columns, dtype=jnp.float32)
    magnitude = jnp.linalg.norm(gram)
    threshold = svt_scale[0] * jnp.sqrt(jnp.trace(gram) / columns)

    def root_turn(counter, state):
        root_part, inverse_root = state
        middle = 1.5 * identity - 0.5 * jnp.dot(inverse_root, root_part, precision=highest)
        return (jnp.dot(root_part, middle, precision=highest), jnp.dot(middle, inverse_root, precision=highest))
    root_part, inverse_root = lax.fori_loop(0, ROOT_STEPS, root_turn, (gram / magnitude, identity))
    root_scale = jnp.sqrt(magnitude)
    shifted = root_scale * root_part - threshold * identity
    signed = shifted / jnp.sqrt(jnp.sum(shifted * shifted) + 1e-06)

    def sign_turn(counter, signed):
        return 1.5 * signed - 0.5 * jnp.dot(signed, jnp.dot(signed, signed, precision=highest), precision=highest)
    signed = lax.fori_loop(0, SIGN_STEPS, sign_turn, signed)
    damping = identity - threshold / root_scale * inverse_root
    return 0.5 * jnp.dot(identity + signed, damping, precision=highest)

def reference(data, sparse, omega, svt_scale, sparse_threshold):
    highest = lax.Precision.HIGHEST
    residual = data - sparse
    sketch = jnp.dot(residual.astype(jnp.bfloat16).astype(jnp.float32), omega.astype(jnp.float32), preferred_element_type=jnp.float32)
    basis = jnp.linalg.qr(sketch)[0]
    projection = jnp.dot(basis.T, residual, precision=highest)
    gram = jnp.dot(projection, projection.T, precision=highest)
    factor = shrink_factor(gram, svt_scale)
    low_rank = jnp.dot(basis, jnp.dot(factor, projection, precision=highest), precision=highest)
    gap = data - low_rank
    sparse_new = jnp.sign(gap) * jnp.maximum(jnp.abs(gap) - sparse_threshold[0], 0.0)
    return (low_rank, sparse_new)
```

```python
import functools

import jax
import jax.numpy as jnp
from jax import lax
from jax.experimental import pallas as pl
from jax.experimental.pallas import tpu as pltpu
from jax.sharding import PartitionSpec as P

ROOT_STEPS = 12
SIGN_STEPS = 12
BASIS_STEPS = 60
CHUNKS = 4
F32 = jnp.float32
BF16 = jnp.bfloat16
MESH = pl.DeviceIdType.MESH


def split(x):
    high = x.astype(BF16)
    return high, (x - high.astype(F32)).astype(BF16)


def dot_split(a, b, dims=((1,), (0,))):
    mul = functools.partial(
        lax.dot_general, dimension_numbers=(dims, ((), ())), preferred_element_type=F32
    )
    (ah, al), (bh, bl) = a, b
    return mul(ah, bh) + (mul(ah, bl) + mul(al, bh))


def mm(a, b):
    return dot_split(split(a), split(b))


def halvings(columns, series):
    steps, rows, place, bit = [], columns, 0, 1
    while bit < series:
        sent = rows // 2 if rows >= 16 else rows
        steps.append((bit, rows, sent, place))
        place += sent
        rows = sent
        bit *= 2
    return steps, place


def gather_kernel(
    series, tm, data_hbm, sparse_hbm, omega_ref, sketch_ref, sums_ref, gram_ref,
    data_v, sparse_v, own, arrived, total, halves, gram_own, gram_in,
    load_sem, sk_send, sk_recv, rs_send, rs_recv, ag_send, ag_recv, g_send, g_recv,
):
    me_s = lax.axis_index("series")
    me_t = lax.axis_index("tm")
    rows, minutes = data_hbm.shape
    columns = omega_ref.shape[1]
    part = rows // CHUNKS
    steps, _ = halvings(columns, series)

    def chunk(c):
        return pl.ds(pl.multiple_of(c * part, part), part)

    def load(c):
        return (
            pltpu.make_async_copy(data_hbm.at[chunk(c)], data_v.at[chunk(c)], load_sem.at[0, c]),
            pltpu.make_async_copy(sparse_hbm.at[chunk(c)], sparse_v.at[chunk(c)], load_sem.at[1, c]),
        )

    for c in range(CHUNKS):
        for copy in load(c):
            copy.start()

    barrier = pltpu.get_barrier_semaphore()
    for d in range(1, tm):
        pl.semaphore_signal(
            barrier, inc=1, device_id=(me_s, lax.rem(me_t + d, tm)), device_id_type=MESH
        )
    for bit, _, _, _ in steps:
        low = lax.rem(me_s // bit, 2)
        pl.semaphore_signal(
            barrier, inc=1, device_id=(me_s + bit - 2 * bit * low, me_t), device_id_type=MESH
        )
    pl.semaphore_wait(barrier, tm - 1 + len(steps))

    def sketch_copy(c, d):
        return pltpu.make_async_remote_copy(
            src_ref=own.at[chunk(c)],
            dst_ref=arrived.at[d - 1, chunk(c)],
            send_sem=sk_send.at[d - 1, c],
            recv_sem=sk_recv.at[d - 1, c],
            device_id=(me_s, lax.rem(me_t + d, tm)),
            device_id_type=MESH,
        )

    def send_sketch(c, carry):
        for copy in load(c):
            copy.wait()
        residual = data_v[chunk(c), :] - sparse_v[chunk(c), :]
        data_v[chunk(c), :] = residual
        own[chunk(c), :] = jnp.dot(
            residual.astype(BF16), omega_ref[...], preferred_element_type=F32
        )
        for d in range(1, tm):
            sketch_copy(c, d).start()
        return carry

    lax.fori_loop(0, CHUNKS, send_sketch, 0)
    total[...] = jnp.zeros_like(total)

    def project(c, carry):
        for d in range(1, tm):
            sketch_copy(c, d).wait_recv()
        sketch = own[chunk(c), :]
        for d in range(1, tm):
            sketch = sketch + arrived[d - 1, chunk(c), :]
        sketch_ref[chunk(c), :] = sketch
        sketch_t = split(sketch.T)
        total[:, :minutes] += dot_split(sketch_t, split(data_v[chunk(c), :]))
        total[:, minutes:] += dot_split(sketch_t, split(sketch))
        return carry

    lax.fori_loop(0, CHUNKS, project, 0)

    start = me_s * 0
    offsets = []
    for turn, (bit, held, sent, place) in enumerate(steps):
        low = lax.rem(me_s // bit, 2)
        other = (me_s + bit - 2 * bit * low, me_t)
        if sent < held:
            keep, give = start + low * sent, start + (1 - low) * sent
        else:
            keep, give = start, start
        copy = pltpu.make_async_remote_copy(
            src_ref=total.at[pl.ds(pl.multiple_of(give, 8), sent)],
            dst_ref=halves.at[pl.ds(place, sent)],
            send_sem=rs_send.at[turn],
            recv_sem=rs_recv.at[turn],
            device_id=other,
            device_id_type=MESH,
        )
        copy.start()
        copy.wait()
        total[pl.ds(pl.multiple_of(keep, 8), sent), :] += halves[pl.ds(place, sent), :]
        offsets.append((keep, other))
        start = keep

    last = steps[-1][2]
    mine = pl.ds(pl.multiple_of(start, 8), last)
    sums_ref[mine, :] = total[mine, :]
    for turn in reversed(range(len(steps))):
        bit, held, sent, _ = steps[turn]
        if sent == held:
            continue
        keep, other = offsets[turn]
        piece = sums_ref.at[pl.ds(pl.multiple_of(keep, 8), sent)]
        copy = pltpu.make_async_remote_copy(
            src_ref=piece,
            dst_ref=piece,
            send_sem=ag_send.at[turn],
            recv_sem=ag_recv.at[turn],
            device_id=other,
            device_id_type=MESH,
        )
        copy.start()
        copy.wait()

    product = split(sums_ref[:, :minutes])
    gram_own[...] = dot_split(product, product, ((1,), (1,)))
    copies = []
    for d in range(1, tm):
        copy = pltpu.make_async_remote_copy(
            src_ref=gram_own,
            dst_ref=gram_in.at[d - 1],
            send_sem=g_send.at[d - 1],
            recv_sem=g_recv.at[d - 1],
            device_id=(me_s, lax.rem(me_t + d, tm)),
            device_id_type=MESH,
        )
        copy.start()
        copies.append(copy)
    for copy in copies:
        copy.wait()
    gram = gram_own[...]
    for d in range(1, tm):
        gram = gram + gram_in[d - 1]
    gram_ref[...] = gram

    def sent_sketch(c, carry):
        for d in range(1, tm):
            sketch_copy(c, d).wait_send()
        return carry

    lax.fori_loop(0, CHUNKS, sent_sketch, 0)


def total_of(x):
    return jnp.sum(jnp.sum(x, axis=1, keepdims=True), axis=0, keepdims=True)


def shrink_into(sums_ref, gram_ref, scale, coef_ref):
    minutes = coef_ref.shape[1]
    columns = gram_ref.shape[0]
    shape = (columns, columns)
    row = lax.broadcasted_iota(jnp.int32, shape, 0)
    col = lax.broadcasted_iota(jnp.int32, shape, 1)
    identity = jnp.where(row == col, 1.0, 0.0).astype(F32)

    def coupled(root, inverse):
        inverse_s, root_s = split(inverse), split(root)
        middle = 1.5 * identity - 0.5 * dot_split(inverse_s, root_s)
        middle_s = split(middle)
        return dot_split(root_s, middle_s), dot_split(middle_s, inverse_s), middle

    first = sums_ref[:, minutes:]
    size = 0.5 * jnp.sqrt(total_of(first * first))

    def basis_on(state):
        counter, error, _, _ = state
        return jnp.logical_and(counter < BASIS_STEPS, error > 2.5e-5)

    def basis_turn(state):
        counter, _, root, inverse = state
        root, inverse, middle = coupled(root, inverse)
        away = middle - identity
        return counter + 1, jnp.sum(away * away), root, inverse

    _, _, _, whiten = lax.while_loop(
        basis_on, basis_turn, (jnp.int32(0), jnp.float32(1.0), first / size, identity)
    )
    whiten = whiten * lax.rsqrt(size)
    whiten_s = split(whiten)
    gram = dot_split(split(dot_split(whiten_s, split(gram_ref[...]))), whiten_s)
    gram = 0.5 * (gram + gram.T)

    magnitude = jnp.sqrt(total_of(gram * gram))
    trace = total_of(gram * identity)
    threshold = scale * jnp.sqrt(trace / columns)
    root, inverse = lax.fori_loop(
        0, ROOT_STEPS, lambda i, s: coupled(*s)[:2], (gram / magnitude, identity)
    )
    root_scale = jnp.sqrt(magnitude)
    shifted = root_scale * root - threshold * identity
    signed = shifted / jnp.sqrt(total_of(shifted * shifted) + 1e-06)

    def sign_turn(i, x):
        x_s = split(x)
        return 1.5 * x - 0.5 * dot_split(x_s, split(dot_split(x_s, x_s)))

    signed = lax.fori_loop(0, SIGN_STEPS, sign_turn, signed)
    factor = 0.5 * mm(identity + signed, identity - threshold / root_scale * inverse)
    inner = mm(dot_split(whiten_s, split(factor)), whiten)
    coef_ref[...] = mm(inner, sums_ref[:, :minutes])


def finish_kernel(sums_ref, gram_ref, scale_ref, cut_ref, sketch_ref, data_ref, low_ref, out_ref, high, rest, coef):
    @pl.when(pl.program_id(0) == 0)
    def _():
        shrink_into(sums_ref, gram_ref, scale_ref[0], coef)
        high[...], rest[...] = split(coef[...])

    low_rank = dot_split(split(sketch_ref[...]), (high[...], rest[...]))
    low_ref[...] = low_rank
    gap = data_ref[...] - low_rank
    size = jnp.maximum(jnp.abs(gap) - cut_ref[0], 0.0)
    out_ref[...] = jnp.where(gap < 0, -size, size)


def on_device(series, tm, data, sparse, omega, svt_scale, sparse_threshold):
    rows, minutes = data.shape
    columns = omega.shape[1]
    wide = minutes + columns
    steps, arrivals = halvings(columns, series)
    turns = len(steps)
    vmem = pl.BlockSpec(memory_space=pltpu.VMEM)
    hbm = pl.BlockSpec(memory_space=pl.ANY)
    dma = pltpu.SemaphoreType.DMA
    sketch, sums, gram = pl.pallas_call(
        functools.partial(gather_kernel, series, tm),
        out_shape=(
            jax.ShapeDtypeStruct((rows, columns), F32),
            jax.ShapeDtypeStruct((columns, wide), F32),
            jax.ShapeDtypeStruct((columns, columns), F32),
        ),
        in_specs=[hbm, hbm, vmem],
        out_specs=(vmem, vmem, vmem),
        scratch_shapes=[
            pltpu.VMEM((rows, minutes), F32),
            pltpu.VMEM((rows, minutes), F32),
            pltpu.VMEM((rows, columns), F32),
            pltpu.VMEM((tm - 1, rows, columns), F32),
            pltpu.VMEM((columns, wide), F32),
            pltpu.VMEM((arrivals, wide), F32),
            pltpu.VMEM((columns, columns), F32),
            pltpu.VMEM((tm - 1, columns, columns), F32),
            dma((2, CHUNKS)),
            dma((tm - 1, CHUNKS)),
            dma((tm - 1, CHUNKS)),
            dma((turns,)),
            dma((turns,)),
            dma((turns,)),
            dma((turns,)),
            dma((tm - 1,)),
            dma((tm - 1,)),
        ],
        compiler_params=pltpu.CompilerParams(
            collective_id=0, has_side_effects=True, vmem_limit_bytes=44 * 2**20
        ),
        name="gather",
    )(data, sparse, omega)
    block = rows // 8
    smem = pl.BlockSpec(memory_space=pltpu.SMEM)
    return pl.pallas_call(
        finish_kernel,
        grid=(rows // block,),
        out_shape=(
            jax.ShapeDtypeStruct((rows, minutes), F32),
            jax.ShapeDtypeStruct((rows, minutes), F32),
        ),
        in_specs=[
            pl.BlockSpec((columns, wide), lambda i: (0, 0)),
            pl.BlockSpec((columns, columns), lambda i: (0, 0)),
            smem,
            smem,
            pl.BlockSpec((block, columns), lambda i: (i, 0)),
            pl.BlockSpec((block, minutes), lambda i: (i, 0)),
        ],
        out_specs=(
            pl.BlockSpec((block, minutes), lambda i: (i, 0)),
            pl.BlockSpec((block, minutes), lambda i: (i, 0)),
        ),
        scratch_shapes=[
            pltpu.VMEM((columns, minutes), BF16),
            pltpu.VMEM((columns, minutes), BF16),
            pltpu.VMEM((columns, minutes), F32),
        ],
        compiler_params=pltpu.CompilerParams(vmem_limit_bytes=44 * 2**20),
        name="finish",
    )(sums, gram, svt_scale, sparse_threshold, sketch, data)


def solution(mesh):
    placed = (P("series", "tm"), P("series", "tm"), P("tm", None), P(), P())
    return jax.shard_map(
        functools.partial(on_device, mesh.shape["series"], mesh.shape["tm"]),
        mesh=mesh,
        in_specs=placed,
        out_specs=(P("series", "tm"), P("series", "tm")),
        check_vma=False,
    )
```

```python
import functools

import jax
import jax.numpy as jnp
from jax import lax
from jax.experimental import pallas as pl
from jax.experimental.pallas import tpu as pltpu
from jax.sharding import PartitionSpec as P

ROOT_STEPS = 12
SIGN_STEPS = 12
QUINTIC_STEPS = 6
CUBIC_STEPS = 4
CHUNKS = 4
LANES = 128
F32 = jnp.float32
BF16 = jnp.bfloat16
MESH = pl.DeviceIdType.MESH


def split(x):
    high = x.astype(BF16)
    return high, (x - high.astype(F32)).astype(BF16)


def dot_split(a, b, dims=((1,), (0,))):
    mul = functools.partial(
        lax.dot_general, dimension_numbers=(dims, ((), ())), preferred_element_type=F32
    )
    (ah, al), (bh, bl) = a, b
    return mul(ah, bh) + (mul(ah, bl) + mul(al, bh))


def mm(a, b):
    return dot_split(split(a), split(b))


def total_of(x):
    return jnp.sum(jnp.sum(x, axis=1, keepdims=True), axis=0, keepdims=True)


def eye(columns):
    shape = (columns, columns)
    row = lax.broadcasted_iota(jnp.int32, shape, 0)
    col = lax.broadcasted_iota(jnp.int32, shape, 1)
    return jnp.where(row == col, 1.0, 0.0).astype(F32)


def apply(root_s, inverse_s, middle):
    middle_s = split(middle)
    return dot_split(root_s, middle_s), dot_split(middle_s, inverse_s)


def cubic(identity, state):
    root_s, inverse_s = split(state[0]), split(state[1])
    return apply(root_s, inverse_s, 1.5 * identity - 0.5 * dot_split(inverse_s, root_s))


def quintic(identity, state):
    root_s, inverse_s = split(state[0]), split(state[1])
    both = dot_split(inverse_s, root_s)
    both_s = split(both)
    middle = 3.4445 * identity - 4.775 * both + 2.0315 * dot_split(both_s, both_s)
    return apply(root_s, inverse_s, middle)


def whitener(first):
    identity = eye(first.shape[0])
    size = jnp.sqrt(total_of(first * first))
    state = (first / size, identity)
    state = lax.fori_loop(0, QUINTIC_STEPS, lambda i, s: quintic(identity, s), state)
    state = lax.fori_loop(0, CUBIC_STEPS, lambda i, s: cubic(identity, s), state)
    return state[1] * lax.rsqrt(size)


def stack(ref, value):
    columns = value.shape[0]
    for k in range(columns // LANES):
        ref[k * columns : (k + 1) * columns, :] = value[:, k * LANES : (k + 1) * LANES]


def unstack(ref, columns):
    return jnp.concatenate(
        [ref[k * columns : (k + 1) * columns, :] for k in range(columns // LANES)], axis=1
    )


def gather_kernel(
    series, tm, data_hbm, sparse_hbm, omega_ref, scale_ref, sketch_ref, high_ref, rest_ref,
    data_v, sparse_v, turned_h, turned_l, own, arrived,
    proj, proj_pair, proj_in, proj_all,
    first, first_pair, first_in, first_all,
    gram, gram_pair, gram_in, gram_tm, gram_all,
    load_sem, sk_sem, proj_sem, first_sem, gram_sem, gram_tm_sem,
):
    me_s = lax.axis_index("series")
    me_t = lax.axis_index("tm")
    core = lax.rem(me_s, 2)
    chip = me_s // 2
    chips = series // 2
    pair = (me_s + 1 - 2 * core, me_t)
    rows, minutes = data_hbm.shape
    columns = omega_ref.shape[1]
    part = rows // CHUNKS

    def chunk(c):
        return pl.ds(pl.multiple_of(c * part, part), part)

    def load(c):
        return (
            pltpu.make_async_copy(data_hbm.at[chunk(c)], data_v.at[chunk(c)], load_sem.at[0, c]),
            pltpu.make_async_copy(sparse_hbm.at[chunk(c)], sparse_v.at[chunk(c)], load_sem.at[1, c]),
        )

    for c in range(CHUNKS):
        for copy in load(c):
            copy.start()

    def peer(d):
        return lax.rem(chip + d, chips)

    barrier = pltpu.get_barrier_semaphore()
    for d in range(1, tm):
        pl.semaphore_signal(
            barrier, inc=1, device_id=(me_s, lax.rem(me_t + d, tm)), device_id_type=MESH
        )
    pl.semaphore_signal(barrier, inc=1, device_id=pair, device_id_type=MESH)
    for d in range(1, chips):
        pl.semaphore_signal(
            barrier, inc=1, device_id=(2 * peer(d) + core, me_t), device_id_type=MESH
        )
    pl.semaphore_wait(barrier, tm - 1 + 1 + chips - 1)

    def remote(src, dst, sem, index, device):
        return pltpu.make_async_remote_copy(
            src_ref=src, dst_ref=dst, send_sem=sem.at[0, index], recv_sem=sem.at[1, index],
            device_id=device, device_id_type=MESH,
        )

    def span(start, size):
        return pl.ds(pl.multiple_of(start, 8), size)

    def pair_out(buf, inbox, sem):
        half = buf.shape[0] // 2
        return [remote(buf.at[span((1 - core) * half, half)], inbox, sem, 0, pair)]

    def pair_add(buf, inbox):
        half = buf.shape[0] // 2
        buf[span(core * half, half), :] += inbox[...]

    def chips_out(buf, inbox, sem):
        half, piece = buf.shape[0] // 2, buf.shape[0] // series
        return [
            remote(
                buf.at[span(core * half + peer(d) * piece, piece)],
                inbox.at[pl.ds((d - 1) * piece, piece)],
                sem, d, (2 * peer(d) + core, me_t),
            )
            for d in range(1, chips)
        ]

    def mine(buf):
        half, piece = buf.shape[0] // 2, buf.shape[0] // series
        return span(core * half + chip * piece, piece)

    def chips_add(buf, inbox):
        piece = buf.shape[0] // series
        value = buf[mine(buf), :]
        for d in range(1, chips):
            value = value + inbox[(d - 1) * piece : d * piece, :]
        return value

    def chips_back(out, sem):
        here = out.at[mine(out)]
        return [
            remote(here, here, sem, chips + d, (2 * peer(d) + core, me_t)) for d in range(1, chips)
        ]

    def pair_back(out, sem):
        half = out.shape[0] // 2
        here = out.at[span(core * half, half)]
        return [remote(here, here, sem, chips, pair)]

    def start(copies):
        for copy in copies:
            copy.start()
        return copies

    def wait(copies):
        for copy in copies:
            copy.wait()

    def sketch_copy(c, d):
        return pltpu.make_async_remote_copy(
            src_ref=own.at[chunk(c)],
            dst_ref=arrived.at[d - 1, chunk(c)],
            send_sem=sk_sem.at[0, d - 1, c],
            recv_sem=sk_sem.at[1, d - 1, c],
            device_id=(me_s, lax.rem(me_t + d, tm)),
            device_id_type=MESH,
        )

    def send_sketch(c, carry):
        for copy in load(c):
            copy.wait()
        residual = data_v[chunk(c), :] - sparse_v[chunk(c), :]
        data_v[chunk(c), :] = residual
        own[chunk(c), :] = jnp.dot(
            residual.astype(BF16), omega_ref[...], preferred_element_type=F32
        )
        for d in range(1, tm):
            sketch_copy(c, d).start()
        return carry

    lax.fori_loop(0, CHUNKS, send_sketch, 0)

    def turn(c, carry):
        turned_h[:, chunk(c)], turned_l[:, chunk(c)] = split(data_v[chunk(c), :].T)
        return carry

    lax.fori_loop(0, CHUNKS, turn, 0)
    proj[...] = jnp.zeros_like(proj)

    def project(c, whole):
        for d in range(1, tm):
            sketch_copy(c, d).wait_recv()
        sketch = own[chunk(c), :]
        for d in range(1, tm):
            sketch = sketch + arrived[d - 1, chunk(c), :]
        sketch_ref[chunk(c), :] = sketch
        sketch_s = split(sketch)
        proj[...] += dot_split((turned_h[:, chunk(c)], turned_l[:, chunk(c)]), sketch_s)
        return whole + dot_split(split(sketch.T), sketch_s)

    stack(first, lax.fori_loop(0, CHUNKS, project, jnp.zeros((columns, columns), F32)))

    first_out = start(pair_out(first, first_pair, first_sem))
    proj_out = start(pair_out(proj, proj_pair, proj_sem))
    wait(first_out)
    pair_add(first, first_pair)
    first_out = start(chips_out(first, first_in, first_sem))
    wait(proj_out)
    pair_add(proj, proj_pair)
    proj_out = start(chips_out(proj, proj_in, proj_sem))
    wait(first_out)
    first_all[mine(first_all), :] = chips_add(first, first_in)
    wait(start(chips_back(first_all, first_sem)))
    wait(start(pair_back(first_all, first_sem)))

    whiten_s = split(whitener(unstack(first_all, columns)))

    wait(proj_out)
    proj_all[mine(proj_all), :] = chips_add(proj, proj_in)
    proj_out = chips_back(proj_all, proj_sem)
    piece_t = split(proj_all[mine(proj_all), :].T)
    stack(gram, dot_split(piece_t, piece_t, ((1,), (1,))))
    wait(start(pair_out(gram, gram_pair, gram_sem)))
    pair_add(gram, gram_pair)
    wait(start(chips_out(gram, gram_in, gram_sem)))
    value = chips_add(gram, gram_in)
    gram[mine(gram), :] = value
    copies = start(
        [
            remote(
                gram.at[mine(gram)], gram_tm.at[d - 1], gram_tm_sem, d - 1,
                (me_s, lax.rem(me_t + d, tm)),
            )
            for d in range(1, tm)
        ]
    )
    wait(copies)
    for d in range(1, tm):
        value = value + gram_tm[d - 1]
    gram_all[mine(gram_all), :] = value
    wait(start(chips_back(gram_all, gram_sem)))
    wait(start(pair_back(gram_all, gram_sem)))
    start(proj_out)

    identity = eye(columns)
    projected = dot_split(
        split(dot_split(whiten_s, split(unstack(gram_all, columns)))), whiten_s
    )
    projected = 0.5 * (projected + projected.T)
    magnitude = jnp.sqrt(total_of(projected * projected))
    threshold = scale_ref[0] * jnp.sqrt(total_of(projected * identity) / columns)
    root, inverse = lax.fori_loop(
        0, ROOT_STEPS, lambda i, s: cubic(identity, s), (projected / magnitude, identity)
    )
    root_scale = jnp.sqrt(magnitude)
    shifted = root_scale * root - threshold * identity
    signed = shifted / jnp.sqrt(total_of(shifted * shifted) + 1e-06)

    wait(proj_out)
    proj_out = start(pair_back(proj_all, proj_sem))

    def sign_turn(i, x):
        x_s = split(x)
        return 1.5 * x - 0.5 * dot_split(x_s, split(dot_split(x_s, x_s)))

    signed = lax.fori_loop(0, SIGN_STEPS, sign_turn, signed)
    factor = 0.5 * mm(identity + signed, identity - threshold / root_scale * inverse)
    inner_s = split(dot_split(split(dot_split(whiten_s, split(factor))), whiten_s))

    wait(proj_out)
    high_ref[...], rest_ref[...] = split(
        dot_split(split(proj_all[...]), inner_s, ((1,), (1,)))
    )

    def sent_sketch(c, carry):
        for d in range(1, tm):
            sketch_copy(c, d).wait_send()
        return carry

    lax.fori_loop(0, CHUNKS, sent_sketch, 0)


def finish_kernel(cut_ref, sketch_ref, high_ref, rest_ref, data_ref, low_ref, out_ref):
    low_rank = dot_split(
        split(sketch_ref[...]), (high_ref[...], rest_ref[...]), ((1,), (1,))
    )
    low_ref[...] = low_rank
    gap = data_ref[...] - low_rank
    size = jnp.maximum(jnp.abs(gap) - cut_ref[0], 0.0)
    out_ref[...] = jnp.where(gap < 0, -size, size)


def on_device(series, tm, data, sparse, omega, svt_scale, sparse_threshold):
    rows, minutes = data.shape
    columns = omega.shape[1]
    chips = series // 2
    stacked = columns * columns // LANES
    vmem = pl.BlockSpec(memory_space=pltpu.VMEM)
    hbm = pl.BlockSpec(memory_space=pltpu.HBM)
    smem = pl.BlockSpec(memory_space=pltpu.SMEM)
    dma = pltpu.SemaphoreType.DMA

    def inboxes(length, width):
        piece = length // series
        return [
            pltpu.VMEM((length, width), F32),
            pltpu.VMEM((length // 2, width), F32),
            pltpu.VMEM(((chips - 1) * piece, width), F32),
        ]

    sketch, high, rest = pl.pallas_call(
        functools.partial(gather_kernel, series, tm),
        out_shape=(
            jax.ShapeDtypeStruct((rows, columns), F32),
            jax.ShapeDtypeStruct((minutes, columns), BF16),
            jax.ShapeDtypeStruct((minutes, columns), BF16),
        ),
        in_specs=[hbm, hbm, vmem, smem],
        out_specs=(vmem, vmem, vmem),
        scratch_shapes=[
            pltpu.VMEM((rows, minutes), F32),
            pltpu.VMEM((rows, minutes), F32),
            pltpu.VMEM((minutes, rows), BF16),
            pltpu.VMEM((minutes, rows), BF16),
            pltpu.VMEM((rows, columns), F32),
            pltpu.VMEM((tm - 1, rows, columns), F32),
            *inboxes(minutes, columns),
            pltpu.VMEM((minutes, columns), F32),
            *inboxes(stacked, LANES),
            pltpu.VMEM((stacked, LANES), F32),
            *inboxes(stacked, LANES),
            pltpu.VMEM((tm - 1, stacked // series, LANES), F32),
            pltpu.VMEM((stacked, LANES), F32),
            dma((2, CHUNKS)),
            dma((2, tm - 1, CHUNKS)),
            dma((2, 2 * chips)),
            dma((2, 2 * chips)),
            dma((2, 2 * chips)),
            dma((2, tm - 1)),
        ],
        compiler_params=pltpu.CompilerParams(
            collective_id=0, has_side_effects=True, vmem_limit_bytes=48 * 2**20
        ),
        name="gather",
    )(data, sparse, omega, svt_scale)
    block = rows // 8
    return pl.pallas_call(
        finish_kernel,
        grid=(rows // block,),
        out_shape=(
            jax.ShapeDtypeStruct((rows, minutes), F32),
            jax.ShapeDtypeStruct((rows, minutes), F32),
        ),
        in_specs=[
            smem,
            pl.BlockSpec((block, columns), lambda i: (i, 0)),
            pl.BlockSpec((minutes, columns), lambda i: (0, 0)),
            pl.BlockSpec((minutes, columns), lambda i: (0, 0)),
            pl.BlockSpec((block, minutes), lambda i: (i, 0)),
        ],
        out_specs=(
            pl.BlockSpec((block, minutes), lambda i: (i, 0)),
            pl.BlockSpec((block, minutes), lambda i: (i, 0)),
        ),
        compiler_params=pltpu.CompilerParams(vmem_limit_bytes=48 * 2**20),
        name="finish",
    )(sparse_threshold, sketch, high, rest, data)


def solution(mesh):
    placed = (P("series", "tm"), P("series", "tm"), P("tm", None), P(), P())
    return jax.shard_map(
        functools.partial(on_device, mesh.shape["series"], mesh.shape["tm"]),
        mesh=mesh,
        in_specs=placed,
        out_specs=(P("series", "tm"), P("series", "tm")),
        check_vma=False,
    )
```

```python
import functools

import jax
import jax.numpy as jnp
from jax import lax
from jax.experimental import pallas as pl
from jax.experimental.pallas import tpu as pltpu
from jax.sharding import PartitionSpec as P

ROOT_STEPS = 12
SIGN_STEPS = 12
QUINTIC_STEPS = 6
CUBIC_STEPS = 4
CHUNKS = 4
LANES = 128
F32 = jnp.float32
BF16 = jnp.bfloat16
MESH = pl.DeviceIdType.MESH


def split(x):
    high = x.astype(BF16)
    return high, (x - high.astype(F32)).astype(BF16)


def dot_split(a, b, dims=((1,), (0,))):
    mul = functools.partial(
        lax.dot_general, dimension_numbers=(dims, ((), ())), preferred_element_type=F32
    )
    (ah, al), (bh, bl) = a, b
    return mul(ah, bh) + (mul(ah, bl) + mul(al, bh))


def mm(a, b):
    return dot_split(split(a), split(b))


def total_of(x):
    return jnp.sum(jnp.sum(x, axis=1, keepdims=True), axis=0, keepdims=True)


def eye(columns):
    shape = (columns, columns)
    row = lax.broadcasted_iota(jnp.int32, shape, 0)
    col = lax.broadcasted_iota(jnp.int32, shape, 1)
    return jnp.where(row == col, 1.0, 0.0).astype(F32)


def apply(root_s, inverse_s, middle):
    middle_s = split(middle)
    return dot_split(root_s, middle_s), dot_split(middle_s, inverse_s)


def cubic(identity, state):
    root_s, inverse_s = split(state[0]), split(state[1])
    return apply(root_s, inverse_s, 1.5 * identity - 0.5 * dot_split(inverse_s, root_s))


def quintic(identity, state):
    root_s, inverse_s = split(state[0]), split(state[1])
    both = dot_split(inverse_s, root_s)
    both_s = split(both)
    middle = 3.4445 * identity - 4.775 * both + 2.0315 * dot_split(both_s, both_s)
    return apply(root_s, inverse_s, middle)


def whiten_turns(first, identity):
    size = jnp.sqrt(total_of(first * first))
    turns = [quintic] * QUINTIC_STEPS + [cubic] * CUBIC_STEPS
    return size, (first / size, identity), turns


def stack(ref, value):
    columns = value.shape[0]
    for k in range(columns // LANES):
        ref[k * columns : (k + 1) * columns, :] = value[:, k * LANES : (k + 1) * LANES]


def unstack(ref, columns):
    return jnp.concatenate(
        [ref[k * columns : (k + 1) * columns, :] for k in range(columns // LANES)], axis=1
    )


def gather_kernel(
    series, tm, data_hbm, sparse_hbm, omega_hbm, scale_ref, sketch_ref, high_ref, rest_ref,
    omega_ref, data_v, sparse_v, turned_h, turned_l, own, arrived,
    proj, proj_pair, proj_in, proj_all,
    first_sum, first, first_pair, first_in, first_all,
    gram, gram_pair, gram_in, gram_tm, gram_all,
    omega_sem, load_sem, sk_sem, proj_sem, back_sem, first_sem, gram_sem, gram_tm_sem,
):
    me_s = lax.axis_index("series")
    me_t = lax.axis_index("tm")
    core = lax.rem(me_s, 2)
    chip = me_s // 2
    chips = series // 2
    pair = (me_s + 1 - 2 * core, me_t)
    rows, minutes = data_hbm.shape
    columns = omega_ref.shape[1]
    part = rows // CHUNKS

    def chunk(c):
        return pl.ds(pl.multiple_of(c * part, part), part)

    def load(c):
        return (
            pltpu.make_async_copy(data_hbm.at[chunk(c)], data_v.at[chunk(c)], load_sem.at[0, c]),
            pltpu.make_async_copy(sparse_hbm.at[chunk(c)], sparse_v.at[chunk(c)], load_sem.at[1, c]),
        )

    omega_load = pltpu.make_async_copy(omega_hbm, omega_ref, omega_sem)
    omega_load.start()
    for c in range(CHUNKS):
        for copy in load(c):
            copy.start()

    def peer(d):
        return lax.rem(chip + d, chips)

    barrier = pltpu.get_barrier_semaphore()
    for d in range(1, tm):
        pl.semaphore_signal(
            barrier, inc=1, device_id=(me_s, lax.rem(me_t + d, tm)), device_id_type=MESH
        )
    pl.semaphore_signal(barrier, inc=1, device_id=pair, device_id_type=MESH)
    for d in range(1, chips):
        pl.semaphore_signal(
            barrier, inc=1, device_id=(2 * peer(d) + core, me_t), device_id_type=MESH
        )
    pl.semaphore_wait(barrier, tm - 1 + 1 + chips - 1)

    def remote(src, dst, sem, index, device):
        return pltpu.make_async_remote_copy(
            src_ref=src, dst_ref=dst, send_sem=sem.at[0, index], recv_sem=sem.at[1, index],
            device_id=device, device_id_type=MESH,
        )

    def span(start, size):
        return pl.ds(pl.multiple_of(start, 8), size)

    def pair_out(buf, inbox, sem):
        half = buf.shape[0] // 2
        return [remote(buf.at[span((1 - core) * half, half)], inbox, sem, 0, pair)]

    def pair_add(buf, inbox):
        half = buf.shape[0] // 2
        buf[span(core * half, half), :] += inbox[...]

    def chips_out(buf, inbox, sem):
        half, piece = buf.shape[0] // 2, buf.shape[0] // series
        return [
            remote(
                buf.at[span(core * half + peer(d) * piece, piece)],
                inbox.at[pl.ds((d - 1) * piece, piece)],
                sem, d, (2 * peer(d) + core, me_t),
            )
            for d in range(1, chips)
        ]

    def mine(buf):
        half, piece = buf.shape[0] // 2, buf.shape[0] // series
        return span(core * half + chip * piece, piece)

    def chips_add(buf, inbox):
        piece = buf.shape[0] // series
        value = buf[mine(buf), :]
        for d in range(1, chips):
            value = value + inbox[(d - 1) * piece : d * piece, :]
        return value

    def chips_back(out, sem):
        here = out.at[mine(out)]
        return [
            remote(here, here, sem, chips + d, (2 * peer(d) + core, me_t)) for d in range(1, chips)
        ]

    def pair_back(out, sem):
        half = out.shape[0] // 2
        here = out.at[span(core * half, half)]
        return [remote(here, here, sem, chips, pair)]

    def start(copies):
        for copy in copies:
            copy.start()
        return copies

    def wait(copies):
        for copy in copies:
            copy.wait()

    def sketch_copy(k, c, d):
        return pltpu.make_async_remote_copy(
            src_ref=own.at[k, chunk(c)],
            dst_ref=arrived.at[d - 1, k, chunk(c)],
            send_sem=sk_sem.at[0, d - 1, k, c],
            recv_sem=sk_sem.at[1, d - 1, k, c],
            device_id=(me_s, lax.rem(me_t + d, tm)),
            device_id_type=MESH,
        )

    blocks = columns // LANES
    omega_load.wait()

    def send_sketch(c, carry):
        for copy in load(c):
            copy.wait()
        residual = data_v[chunk(c), :] - sparse_v[chunk(c), :]
        data_v[chunk(c), :] = residual
        sketch = jnp.dot(residual.astype(BF16), omega_ref[...], preferred_element_type=F32)
        for k in range(blocks):
            own[k, chunk(c), :] = sketch[:, k * LANES : (k + 1) * LANES]
        for d in range(1, tm):
            sketch_copy(0, c, d).start()
        return carry

    lax.fori_loop(0, CHUNKS, send_sketch, 0)

    def send_rest(c, carry):
        for k in range(1, blocks):
            for d in range(1, tm):
                sketch_copy(k, c, d).start()
        return carry

    lax.fori_loop(0, CHUNKS, send_rest, 0)

    def turn(c, carry):
        turned_h[:, chunk(c)], turned_l[:, chunk(c)] = split(data_v[chunk(c), :].T)
        return carry

    lax.fori_loop(0, CHUNKS, turn, 0)
    proj[...] = jnp.zeros_like(proj)

    def project(k):
        lanes = pl.ds(k * LANES, LANES)

        def turn_of(c, carry):
            for d in range(1, tm):
                sketch_copy(k, c, d).wait_recv()
            sketch = own[k, chunk(c), :]
            for d in range(1, tm):
                sketch = sketch + arrived[d - 1, k, chunk(c), :]
            sketch_ref[chunk(c), lanes] = sketch
            sketch_s = split(sketch)
            proj[k] += dot_split((turned_h[:, chunk(c)], turned_l[:, chunk(c)]), sketch_s)
            if k == blocks - 1:
                every = sketch_ref[chunk(c), :]
                first_sum[...] += dot_split(split(every.T), split(every))
            return carry

        lax.fori_loop(0, CHUNKS, turn_of, 0)

    first_sum[...] = jnp.zeros_like(first_sum)
    proj_out = []
    for k in range(blocks - 1):
        project(k)
        wait(start(pair_out(proj.at[k], proj_pair.at[k], proj_sem.at[k])))
        pair_add(proj.at[k], proj_pair.at[k])
        proj_out += start(chips_out(proj.at[k], proj_in.at[k], proj_sem.at[k]))
    project(blocks - 1)
    stack(first, first_sum[...])

    tail = blocks - 1
    first_out = start(pair_out(first, first_pair, first_sem))
    tail_out = start(pair_out(proj.at[tail], proj_pair.at[tail], proj_sem.at[tail]))
    wait(first_out)
    pair_add(first, first_pair)
    first_out = start(chips_out(first, first_in, first_sem))
    wait(tail_out)
    pair_add(proj.at[tail], proj_pair.at[tail])
    proj_out += start(chips_out(proj.at[tail], proj_in.at[tail], proj_sem.at[tail]))
    wait(first_out)
    first_all[mine(first_all), :] = chips_add(first, first_in)
    wait(start(chips_back(first_all, first_sem)))
    wait(start(pair_back(first_all, first_sem)))

    wait(proj_out)
    for k in range(blocks):
        proj_all[mine(proj_all), pl.ds(k * LANES, LANES)] = chips_add(proj.at[k], proj_in.at[k])
    piece_t = split(proj_all[mine(proj_all), :].T)
    stack(gram, dot_split(piece_t, piece_t, ((1,), (1,))))

    identity = eye(columns)
    size, state, turns = whiten_turns(unstack(first_all, columns), identity)
    share = -(-len(turns) // 5)

    def whiten_some(state, hop):
        for turn_now in turns[hop * share : (hop + 1) * share]:
            state = turn_now(identity, state)
        return state

    copies = start(pair_out(gram, gram_pair, gram_sem))
    state = whiten_some(state, 0)
    wait(copies)
    pair_add(gram, gram_pair)
    copies = start(chips_out(gram, gram_in, gram_sem))
    state = whiten_some(state, 1)
    wait(copies)
    value = chips_add(gram, gram_in)
    gram[mine(gram), :] = value
    copies = start(
        [
            remote(
                gram.at[mine(gram)], gram_tm.at[d - 1], gram_tm_sem, d - 1,
                (me_s, lax.rem(me_t + d, tm)),
            )
            for d in range(1, tm)
        ]
    )
    state = whiten_some(state, 2)
    wait(copies)
    for d in range(1, tm):
        value = value + gram_tm[d - 1]
    gram_all[mine(gram_all), :] = value
    copies = start(chips_back(gram_all, gram_sem))
    proj_out = start(chips_back(proj_all, back_sem))
    state = whiten_some(state, 3)
    wait(copies)
    copies = start(pair_back(gram_all, gram_sem))
    state = whiten_some(state, 4)
    whiten_s = split(state[1] * lax.rsqrt(size))
    wait(copies)

    projected = dot_split(
        split(dot_split(whiten_s, split(unstack(gram_all, columns)))), whiten_s
    )
    projected = 0.5 * (projected + projected.T)
    magnitude = jnp.sqrt(total_of(projected * projected))
    threshold = scale_ref[0] * jnp.sqrt(total_of(projected * identity) / columns)
    root, inverse = lax.fori_loop(
        0, ROOT_STEPS, lambda i, s: cubic(identity, s), (projected / magnitude, identity)
    )
    root_scale = jnp.sqrt(magnitude)
    shifted = root_scale * root - threshold * identity
    signed = shifted / jnp.sqrt(total_of(shifted * shifted) + 1e-06)

    wait(proj_out)
    proj_out = start(pair_back(proj_all, back_sem))

    def sign_turn(i, x):
        x_s = split(x)
        return 1.5 * x - 0.5 * dot_split(x_s, split(dot_split(x_s, x_s)))

    signed = lax.fori_loop(0, SIGN_STEPS, sign_turn, signed)
    factor = 0.5 * mm(identity + signed, identity - threshold / root_scale * inverse)
    inner_s = split(dot_split(split(dot_split(whiten_s, split(factor))), whiten_s))

    wait(proj_out)
    high_ref[...], rest_ref[...] = split(
        dot_split(inner_s, split(proj_all[...]), ((1,), (1,)))
    )

    def sent_sketch(c, carry):
        for k in range(blocks):
            for d in range(1, tm):
                sketch_copy(k, c, d).wait_send()
        return carry

    lax.fori_loop(0, CHUNKS, sent_sketch, 0)


def finish_kernel(cut_ref, sketch_ref, high_ref, rest_ref, data_ref, low_ref, out_ref):
    low_rank = dot_split(
        split(sketch_ref[...]), (high_ref[...], rest_ref[...])
    )
    low_ref[...] = low_rank
    gap = data_ref[...] - low_rank
    size = jnp.maximum(jnp.abs(gap) - cut_ref[0], 0.0)
    out_ref[...] = jnp.where(gap < 0, -size, size)


def on_device(series, tm, data, sparse, omega, svt_scale, sparse_threshold):
    rows, minutes = data.shape
    columns = omega.shape[1]
    chips = series // 2
    stacked = columns * columns // LANES
    vmem = pl.BlockSpec(memory_space=pltpu.VMEM)
    hbm = pl.BlockSpec(memory_space=pltpu.HBM)
    smem = pl.BlockSpec(memory_space=pltpu.SMEM)
    dma = pltpu.SemaphoreType.DMA

    blocks = columns // LANES

    def inboxes(*shape):
        length = shape[-1]
        return [
            pltpu.VMEM((*shape[:-1], size, LANES), F32)
            for size in (length, length // 2, (chips - 1) * (length // series))
        ]

    sketch, high, rest = pl.pallas_call(
        functools.partial(gather_kernel, series, tm),
        out_shape=(
            jax.ShapeDtypeStruct((rows, columns), F32),
            jax.ShapeDtypeStruct((columns, minutes), BF16),
            jax.ShapeDtypeStruct((columns, minutes), BF16),
        ),
        in_specs=[hbm, hbm, hbm, smem],
        out_specs=(vmem, vmem, vmem),
        scratch_shapes=[
            pltpu.VMEM((minutes, columns), BF16),
            pltpu.VMEM((rows, minutes), F32),
            pltpu.VMEM((rows, minutes), F32),
            pltpu.VMEM((minutes, rows), BF16),
            pltpu.VMEM((minutes, rows), BF16),
            pltpu.VMEM((blocks, rows, LANES), F32),
            pltpu.VMEM((tm - 1, blocks, rows, LANES), F32),
            *inboxes(blocks, minutes),
            pltpu.VMEM((minutes, columns), F32),
            pltpu.VMEM((columns, columns), F32),
            *inboxes(stacked),
            pltpu.VMEM((stacked, LANES), F32),
            *inboxes(stacked),
            pltpu.VMEM((tm - 1, stacked // series, LANES), F32),
            pltpu.VMEM((stacked, LANES), F32),
            dma,
            dma((2, CHUNKS)),
            dma((2, tm - 1, blocks, CHUNKS)),
            dma((blocks, 2, 2 * chips)),
            dma((2, 2 * chips)),
            dma((2, 2 * chips)),
            dma((2, 2 * chips)),
            dma((2, tm - 1)),
        ],
        compiler_params=pltpu.CompilerParams(
            collective_id=0, has_side_effects=True, vmem_limit_bytes=48 * 2**20
        ),
        name="gather",
    )(data, sparse, omega, svt_scale)
    block = rows // 8
    return pl.pallas_call(
        finish_kernel,
        grid=(rows // block,),
        out_shape=(
            jax.ShapeDtypeStruct((rows, minutes), F32),
            jax.ShapeDtypeStruct((rows, minutes), F32),
        ),
        in_specs=[
            smem,
            pl.BlockSpec((block, columns), lambda i: (i, 0)),
            pl.BlockSpec((columns, minutes), lambda i: (0, 0)),
            pl.BlockSpec((columns, minutes), lambda i: (0, 0)),
            pl.BlockSpec((block, minutes), lambda i: (i, 0)),
        ],
        out_specs=(
            pl.BlockSpec((block, minutes), lambda i: (i, 0)),
            pl.BlockSpec((block, minutes), lambda i: (i, 0)),
        ),
        compiler_params=pltpu.CompilerParams(vmem_limit_bytes=48 * 2**20),
        name="finish",
    )(sparse_threshold, sketch, high, rest, data)


def solution(mesh):
    placed = (P("series", "tm"), P("series", "tm"), P("tm", None), P(), P())
    return jax.shard_map(
        functools.partial(on_device, mesh.shape["series"], mesh.shape["tm"]),
        mesh=mesh,
        in_specs=placed,
        out_specs=(P("series", "tm"), P("series", "tm")),
        check_vma=False,
    )
```

```python
import functools

import jax
import jax.numpy as jnp
from jax import lax
from jax.experimental import pallas as pl
from jax.experimental.pallas import tpu as pltpu
from jax.sharding import PartitionSpec as P

ROOT_STEPS = 12
SIGN_STEPS = 12
QUINTIC_STEPS = 6
CUBIC_STEPS = 4
CHUNKS = 4
LANES = 128
F32 = jnp.float32
BF16 = jnp.bfloat16
MESH = pl.DeviceIdType.MESH


def split(x):
    high = x.astype(BF16)
    return high, (x - high.astype(F32)).astype(BF16)


def dot_split(a, b, dims=((1,), (0,))):
    mul = functools.partial(
        lax.dot_general, dimension_numbers=(dims, ((), ())), preferred_element_type=F32
    )
    (ah, al), (bh, bl) = a, b
    return mul(ah, bh) + (mul(ah, bl) + mul(al, bh))


def mm(a, b):
    return dot_split(split(a), split(b))


def total_of(x):
    return jnp.sum(jnp.sum(x, axis=1, keepdims=True), axis=0, keepdims=True)


def eye(columns):
    shape = (columns, columns)
    row = lax.broadcasted_iota(jnp.int32, shape, 0)
    col = lax.broadcasted_iota(jnp.int32, shape, 1)
    return jnp.where(row == col, 1.0, 0.0).astype(F32)


def apply(root_s, inverse_s, middle):
    middle_s = split(middle)
    return dot_split(root_s, middle_s), dot_split(middle_s, inverse_s)


def cubic(identity, state):
    root_s, inverse_s = split(state[0]), split(state[1])
    return apply(root_s, inverse_s, 1.5 * identity - 0.5 * dot_split(inverse_s, root_s))


def quintic(identity, state):
    root_s, inverse_s = split(state[0]), split(state[1])
    both = dot_split(inverse_s, root_s)
    both_s = split(both)
    middle = 3.4445 * identity - 4.775 * both + 2.0315 * dot_split(both_s, both_s)
    return apply(root_s, inverse_s, middle)


def whiten_turns(first, identity):
    size = jnp.sqrt(total_of(first * first))
    turns = [quintic] * QUINTIC_STEPS + [cubic] * CUBIC_STEPS
    return size, (first / size, identity), turns


def stack(ref, value):
    columns = value.shape[0]
    for k in range(columns // LANES):
        ref[k * columns : (k + 1) * columns, :] = value[:, k * LANES : (k + 1) * LANES]


def unstack(ref, columns):
    return jnp.concatenate(
        [ref[k * columns : (k + 1) * columns, :] for k in range(columns // LANES)], axis=1
    )


def gather_kernel(
    series, tm, data_hbm, sparse_hbm, omega_hbm, scale_ref, sketch_ref, high_ref, rest_ref,
    omega_ref, data_v, sparse_v, turned_h, turned_l, own, arrived,
    proj, proj_pair, proj_in, proj_all,
    first_sum, first, first_pair, first_in, first_all,
    gram, gram_pair, gram_in, gram_tm, gram_all,
    omega_sem, load_sem, sk_sem, proj_sem, back_sem, first_sem, gram_sem, gram_tm_sem,
):
    me_s = lax.axis_index("series")
    me_t = lax.axis_index("tm")
    core = lax.rem(me_s, 2)
    chip = me_s // 2
    chips = series // 2
    pair = (me_s + 1 - 2 * core, me_t)
    rows, minutes = data_hbm.shape
    columns = omega_ref.shape[1]
    part = rows // CHUNKS

    def chunk(c):
        return pl.ds(pl.multiple_of(c * part, part), part)

    def load(c):
        return (
            pltpu.make_async_copy(data_hbm.at[chunk(c)], data_v.at[chunk(c)], load_sem.at[0, c]),
            pltpu.make_async_copy(sparse_hbm.at[chunk(c)], sparse_v.at[chunk(c)], load_sem.at[1, c]),
        )

    omega_load = pltpu.make_async_copy(omega_hbm, omega_ref, omega_sem)
    omega_load.start()
    for c in range(CHUNKS):
        for copy in load(c):
            copy.start()

    def peer(d):
        return lax.rem(chip + d, chips)

    barrier = pltpu.get_barrier_semaphore()
    for d in range(1, tm):
        pl.semaphore_signal(
            barrier, inc=1, device_id=(me_s, lax.rem(me_t + d, tm)), device_id_type=MESH
        )
    pl.semaphore_signal(barrier, inc=1, device_id=pair, device_id_type=MESH)
    for d in range(1, chips):
        pl.semaphore_signal(
            barrier, inc=1, device_id=(2 * peer(d) + core, me_t), device_id_type=MESH
        )
    pl.semaphore_wait(barrier, tm - 1 + 1 + chips - 1)

    def remote(src, dst, sem, index, device):
        return pltpu.make_async_remote_copy(
            src_ref=src, dst_ref=dst, send_sem=sem.at[0, index], recv_sem=sem.at[1, index],
            device_id=device, device_id_type=MESH,
        )

    def span(start, size):
        return pl.ds(pl.multiple_of(start, 8), size)

    def pair_out(buf, inbox, sem):
        half = buf.shape[0] // 2
        return [remote(buf.at[span((1 - core) * half, half)], inbox, sem, 0, pair)]

    def pair_add(buf, inbox):
        half = buf.shape[0] // 2
        buf[span(core * half, half), :] += inbox[...]

    def chips_out(buf, inbox, sem):
        half, piece = buf.shape[0] // 2, buf.shape[0] // series
        return [
            remote(
                buf.at[span(core * half + peer(d) * piece, piece)],
                inbox.at[pl.ds((d - 1) * piece, piece)],
                sem, d, (2 * peer(d) + core, me_t),
            )
            for d in range(1, chips)
        ]

    def mine(buf):
        half, piece = buf.shape[0] // 2, buf.shape[0] // series
        return span(core * half + chip * piece, piece)

    def chips_add(buf, inbox):
        piece = buf.shape[0] // series
        value = buf[mine(buf), :]
        for d in range(1, chips):
            value = value + inbox[(d - 1) * piece : d * piece, :]
        return value

    def chips_back(out, sem):
        here = out.at[mine(out)]
        return [
            remote(here, here, sem, chips + d, (2 * peer(d) + core, me_t)) for d in range(1, chips)
        ]

    def pair_back(out, sem):
        half = out.shape[0] // 2
        here = out.at[span(core * half, half)]
        return [remote(here, here, sem, chips, pair)]

    def start(copies):
        for copy in copies:
            copy.start()
        return copies

    def wait(copies):
        for copy in copies:
            copy.wait()

    def sketch_copy(k, c, d):
        return pltpu.make_async_remote_copy(
            src_ref=own.at[k, chunk(c)],
            dst_ref=arrived.at[d - 1, k, chunk(c)],
            send_sem=sk_sem.at[0, d - 1, k, c],
            recv_sem=sk_sem.at[1, d - 1, k, c],
            device_id=(me_s, lax.rem(me_t + d, tm)),
            device_id_type=MESH,
        )

    blocks = columns // LANES
    omega_load.wait()

    def send_sketch(c, carry):
        for copy in load(c):
            copy.wait()
        residual = data_v[chunk(c), :] - sparse_v[chunk(c), :]
        data_v[chunk(c), :] = residual
        sketch = jnp.dot(residual.astype(BF16), omega_ref[...], preferred_element_type=F32)
        for k in range(blocks):
            own[k, chunk(c), :] = sketch[:, k * LANES : (k + 1) * LANES]
        for d in range(1, tm):
            sketch_copy(0, c, d).start()
        return carry

    lax.fori_loop(0, CHUNKS, send_sketch, 0)

    def send_rest(c, carry):
        for k in range(1, blocks):
            for d in range(1, tm):
                sketch_copy(k, c, d).start()
        return carry

    lax.fori_loop(0, CHUNKS, send_rest, 0)

    def turn(c, carry):
        turned_h[:, chunk(c)], turned_l[:, chunk(c)] = split(data_v[chunk(c), :].T)
        return carry

    lax.fori_loop(0, CHUNKS, turn, 0)
    proj[...] = jnp.zeros_like(proj)

    def project(k):
        lanes = pl.ds(k * LANES, LANES)

        def turn_of(c, carry):
            for d in range(1, tm):
                sketch_copy(k, c, d).wait_recv()
            sketch = own[k, chunk(c), :]
            for d in range(1, tm):
                sketch = sketch + arrived[d - 1, k, chunk(c), :]
            sketch_ref[chunk(c), lanes] = sketch
            sketch_s = split(sketch)
            proj[k] += dot_split((turned_h[:, chunk(c)], turned_l[:, chunk(c)]), sketch_s)
            if k == blocks - 1:
                every = sketch_ref[chunk(c), :]
                first_sum[...] += dot_split(split(every.T), split(every))
            return carry

        lax.fori_loop(0, CHUNKS, turn_of, 0)

    first_sum[...] = jnp.zeros_like(first_sum)
    proj_out = []
    for k in range(blocks - 1):
        project(k)
        wait(start(pair_out(proj.at[k], proj_pair.at[k], proj_sem.at[k])))
        pair_add(proj.at[k], proj_pair.at[k])
        proj_out += start(chips_out(proj.at[k], proj_in.at[k], proj_sem.at[k]))
    project(blocks - 1)
    stack(first, first_sum[...])

    tail = blocks - 1
    tail_out = start(pair_out(proj.at[tail], proj_pair.at[tail], proj_sem.at[tail]))
    first_out = start(pair_out(first, first_pair, first_sem))
    wait(tail_out)
    pair_add(proj.at[tail], proj_pair.at[tail])
    proj_out += start(chips_out(proj.at[tail], proj_in.at[tail], proj_sem.at[tail]))
    wait(first_out)
    pair_add(first, first_pair)
    first_out = start(chips_out(first, first_in, first_sem))

    wait(proj_out)
    for k in range(blocks):
        proj_all[mine(proj_all), pl.ds(k * LANES, LANES)] = chips_add(proj.at[k], proj_in.at[k])
    piece_t = split(proj_all[mine(proj_all), :].T)
    stack(gram, dot_split(piece_t, piece_t, ((1,), (1,))))

    copies = start(pair_out(gram, gram_pair, gram_sem))
    wait(first_out)
    first_all[mine(first_all), :] = chips_add(first, first_in)
    first_out = start(chips_back(first_all, first_sem))
    wait(copies)
    pair_add(gram, gram_pair)
    copies = start(chips_out(gram, gram_in, gram_sem))
    wait(first_out)
    wait(start(pair_back(first_all, first_sem)))

    identity = eye(columns)
    size, state, turns = whiten_turns(unstack(first_all, columns), identity)
    share = -(-len(turns) // 4)

    def whiten_some(state, hop):
        for turn_now in turns[max(0, hop * share - 2) : (hop + 1) * share - 2]:
            state = turn_now(identity, state)
        return state

    state = whiten_some(state, 0)
    wait(copies)
    value = chips_add(gram, gram_in)
    gram[mine(gram), :] = value
    copies = start(
        [
            remote(
                gram.at[mine(gram)], gram_tm.at[d - 1], gram_tm_sem, d - 1,
                (me_s, lax.rem(me_t + d, tm)),
            )
            for d in range(1, tm)
        ]
    )
    state = whiten_some(state, 1)
    wait(copies)
    for d in range(1, tm):
        value = value + gram_tm[d - 1]
    gram_all[mine(gram_all), :] = value
    copies = start(chips_back(gram_all, gram_sem))
    state = whiten_some(state, 2)
    wait(copies)
    copies = start(pair_back(gram_all, gram_sem))
    proj_out = start(chips_back(proj_all, back_sem))
    state = whiten_some(state, 3)
    whiten_s = split(state[1] * lax.rsqrt(size))
    wait(copies)

    projected = dot_split(
        split(dot_split(whiten_s, split(unstack(gram_all, columns)))), whiten_s
    )
    projected = 0.5 * (projected + projected.T)
    magnitude = jnp.sqrt(total_of(projected * projected))
    threshold = scale_ref[0] * jnp.sqrt(total_of(projected * identity) / columns)
    root, inverse = lax.fori_loop(
        0, ROOT_STEPS, lambda i, s: cubic(identity, s), (projected / magnitude, identity)
    )
    root_scale = jnp.sqrt(magnitude)
    shifted = root_scale * root - threshold * identity
    signed = shifted / jnp.sqrt(total_of(shifted * shifted) + 1e-06)

    wait(proj_out)
    proj_out = start(pair_back(proj_all, back_sem))

    def sign_turn(i, x):
        x_s = split(x)
        return 1.5 * x - 0.5 * dot_split(x_s, split(dot_split(x_s, x_s)))

    signed = lax.fori_loop(0, SIGN_STEPS, sign_turn, signed)
    factor = 0.5 * mm(identity + signed, identity - threshold / root_scale * inverse)
    inner_s = split(dot_split(split(dot_split(whiten_s, split(factor))), whiten_s))

    wait(proj_out)
    high_ref[...], rest_ref[...] = split(
        dot_split(inner_s, split(proj_all[...]), ((1,), (1,)))
    )

    def sent_sketch(c, carry):
        for k in range(blocks):
            for d in range(1, tm):
                sketch_copy(k, c, d).wait_send()
        return carry

    lax.fori_loop(0, CHUNKS, sent_sketch, 0)


def finish_kernel(cut_ref, sketch_ref, high_ref, rest_ref, data_ref, low_ref, out_ref):
    low_rank = dot_split(
        split(sketch_ref[...]), (high_ref[...], rest_ref[...])
    )
    low_ref[...] = low_rank
    gap = data_ref[...] - low_rank
    size = jnp.maximum(jnp.abs(gap) - cut_ref[0], 0.0)
    out_ref[...] = jnp.where(gap < 0, -size, size)


def on_device(series, tm, data, sparse, omega, svt_scale, sparse_threshold):
    rows, minutes = data.shape
    columns = omega.shape[1]
    chips = series // 2
    stacked = columns * columns // LANES
    vmem = pl.BlockSpec(memory_space=pltpu.VMEM)
    hbm = pl.BlockSpec(memory_space=pltpu.HBM)
    smem = pl.BlockSpec(memory_space=pltpu.SMEM)
    dma = pltpu.SemaphoreType.DMA

    blocks = columns // LANES

    def inboxes(*shape):
        length = shape[-1]
        return [
            pltpu.VMEM((*shape[:-1], size, LANES), F32)
            for size in (length, length // 2, (chips - 1) * (length // series))
        ]

    sketch, high, rest = pl.pallas_call(
        functools.partial(gather_kernel, series, tm),
        out_shape=(
            jax.ShapeDtypeStruct((rows, columns), F32),
            jax.ShapeDtypeStruct((columns, minutes), BF16),
            jax.ShapeDtypeStruct((columns, minutes), BF16),
        ),
        in_specs=[hbm, hbm, hbm, smem],
        out_specs=(vmem, vmem, vmem),
        scratch_shapes=[
            pltpu.VMEM((minutes, columns), BF16),
            pltpu.VMEM((rows, minutes), F32),
            pltpu.VMEM((rows, minutes), F32),
            pltpu.VMEM((minutes, rows), BF16),
            pltpu.VMEM((minutes, rows), BF16),
            pltpu.VMEM((blocks, rows, LANES), F32),
            pltpu.VMEM((tm - 1, blocks, rows, LANES), F32),
            *inboxes(blocks, minutes),
            pltpu.VMEM((minutes, columns), F32),
            pltpu.VMEM((columns, columns), F32),
            *inboxes(stacked),
            pltpu.VMEM((stacked, LANES), F32),
            *inboxes(stacked),
            pltpu.VMEM((tm - 1, stacked // series, LANES), F32),
            pltpu.VMEM((stacked, LANES), F32),
            dma,
            dma((2, CHUNKS)),
            dma((2, tm - 1, blocks, CHUNKS)),
            dma((blocks, 2, 2 * chips)),
            dma((2, 2 * chips)),
            dma((2, 2 * chips)),
            dma((2, 2 * chips)),
            dma((2, tm - 1)),
        ],
        compiler_params=pltpu.CompilerParams(
            collective_id=0, has_side_effects=True, vmem_limit_bytes=48 * 2**20
        ),
        name="gather",
    )(data, sparse, omega, svt_scale)
    block = rows // 4
    return pl.pallas_call(
        finish_kernel,
        grid=(rows // block,),
        out_shape=(
            jax.ShapeDtypeStruct((rows, minutes), F32),
            jax.ShapeDtypeStruct((rows, minutes), F32),
        ),
        in_specs=[
            smem,
            pl.BlockSpec((block, columns), lambda i: (i, 0)),
            pl.BlockSpec((columns, minutes), lambda i: (0, 0)),
            pl.BlockSpec((columns, minutes), lambda i: (0, 0)),
            pl.BlockSpec((block, minutes), lambda i: (i, 0)),
        ],
        out_specs=(
            pl.BlockSpec((block, minutes), lambda i: (i, 0)),
            pl.BlockSpec((block, minutes), lambda i: (i, 0)),
        ),
        compiler_params=pltpu.CompilerParams(vmem_limit_bytes=48 * 2**20),
        name="finish",
    )(sparse_threshold, sketch, high, rest, data)


def solution(mesh):
    placed = (P("series", "tm"), P("series", "tm"), P("tm", None), P(), P())
    return jax.shard_map(
        functools.partial(on_device, mesh.shape["series"], mesh.shape["tm"]),
        mesh=mesh,
        in_specs=placed,
        out_specs=(P("series", "tm"), P("series", "tm")),
        check_vma=False,
    )
```
